32 devices in a mesh: tiles: 8 (over z, x), pair: 4 (over y, core).
Axes of the slice: x: 2, y: 2, z: 4, core: 2. Of those that a mesh axis runs over, the one named last changes fastest.
Arguments:
- t2: bfloat16 [256, 16, 4096], P('tiles', None, 'pair'), may hold values from -6 to 6
- v_plus: bfloat16 [8, 64, 16, 2048], P('tiles'), may hold values from -0.1875 to 0.1875
- v_minus: bfloat16 [8, 64, 16, 2048], P('tiles'), may hold values from -0.1875 to 0.1875
- partner: int32 [4096], P('pair'), may hold values from 0 to 1023, as said below
- win_tile: int32 [8, 64], replicated, may hold values from 0 to 255, as said below
- win_count: int32 [8], replicated, may hold values from 48 to 64, as said below
Outputs:
- ladder: bfloat16 [4096, 16384], P('pair', 'tiles')
The draws below stay inside these ranges and needn't reach their ends.
Inputs may be any that keep to these rules, and one draw needn't show every extreme that they name: `partner`: each block of 1024 entries is a permutation of 0 to 1023, and blocks 2h and 2h + 1 are inverse to each other. `win_tile`: the live entries of one owner's list name distinct tiles; at most 8 of them lie among one index of tiles' 32 tiles (tiles k * 32 to (k + 1) * 32 - 1), and some owner takes exactly 8 from one index in every draw. Entries past the live count name tiles too. `win_count`: some owner has exactly 64 live slots.
All inputs are finite; a program needn't handle non-finite values.
Results may differ from the reference program's by a relative error of at most 0.0052.
Values may be sent and summed in bfloat16 or wider, within the bound.
A program may use at most 128 MiB of HBM per device.

```python
import jax
import jax.numpy as jnp
from jax import lax

OP_DEV = 1024
TW = 16
WIN = 64
SAB = 2048
TILES_IN = 32
CAP = 8
NT = 256
OPAIRS = 4096
N_TILES = 8
N_PAIR = 4


def window_lists(key):
    key_count, key_second, key_order, key_full, key_shuffle, key_start = jax.random.split(key, 6)
    span_size = WIN // 4
    first_draw = jax.random.randint(key_count, (N_TILES,), 0, span_size + 1)
    second_draw = jax.random.randint(key_second, (N_TILES,), 0, span_size + 1)
    counts = WIN - jnp.minimum(first_draw, second_draw)
    full_owner = jax.random.randint(key_full, (), 0, N_TILES)
    counts = jnp.where(jnp.arange(N_TILES) == full_owner, WIN, counts).astype(jnp.int32)
    source_orders = jax.vmap(lambda k: jax.random.permutation(k, N_TILES))(jax.random.split(key_order, N_TILES))
    start_tiles = jax.random.randint(key_start, (N_TILES, N_TILES), 0, TILES_IN)
    slot_block = jnp.arange(WIN) // CAP
    in_block = jnp.arange(WIN) % CAP
    sources = source_orders[:, slot_block]
    offsets = (start_tiles[:, slot_block] + in_block[None, :]) % TILES_IN
    tiles = sources * TILES_IN + offsets
    scores = jax.random.randint(key_shuffle, (N_TILES, WIN), 0, 4096) * WIN + jnp.arange(WIN)[None, :]
    scores = scores + jnp.where(jnp.arange(WIN)[None, :] < counts[:, None], 0, 2 ** 24)
    shuffle = jnp.argsort(scores, axis=1)
    tiles = jnp.take_along_axis(tiles, shuffle, axis=1)
    return (tiles.astype(jnp.int32), counts)


def draw_win_tile(key, part):
    return window_lists(key)[0]


def draw_win_count(key, part):
    return window_lists(key)[1]


def draw_partner(key, part):
    key = jax.random.fold_in(key, 7)
    half_count = N_PAIR // 2
    orders = jax.vmap(lambda k: jax.random.permutation(k, OP_DEV))(jax.random.split(key, half_count))
    inverse = jnp.argsort(orders, axis=1)
    stacked = jnp.stack([orders, inverse], axis=1)
    return stacked.reshape(half_count * 2 * OP_DEV).astype(jnp.int32)


def shard_levels(own_key, dims, pieces, low, top_value):
    def one(dim, shards_of):
        draws = jax.random.uniform(jax.random.fold_in(jax.random.fold_in(own_key, 6), dim), (shards_of,), jnp.float32, low / len(pieces), top_value / len(pieces))
        return jnp.repeat(jnp.exp(draws), dims[dim] // shards_of).reshape((-1,) + (1,) * (len(dims) - dim - 1))

    loudness = one(*pieces[0])
    for cut in pieces[1:]:
        loudness = loudness * one(*cut)
    return loudness


def bell_draw(rng, extent, scale, reach, cuts=(), held_as=jnp.bfloat16):
    entries = jax.random.normal(rng, extent, jnp.float32) * scale
    if len(cuts) > 0:
        entries = shard_levels(rng, extent, cuts, -0.22, 0.18) * entries
    return jnp.clip(entries, min=-reach, max=reach).astype(held_as)


def setup_inputs(seed: int = 0) -> dict:
    streams_of = jax.random.split(jax.random.key(seed), 7)
    t2 = bell_draw(streams_of[0], (NT, TW, OPAIRS), 1.0, 6.0, ((0, 8), (2, 4)))
    v_plus = bell_draw(streams_of[1], (N_TILES, WIN, TW, SAB), (WIN * TW) ** -0.5, 0.1875, ((0, 8),))
    v_minus = bell_draw(streams_of[2], (N_TILES, WIN, TW, SAB), (WIN * TW) ** -0.5, 0.1875, ((0, 8),))
    partner = draw_partner(jax.random.fold_in(streams_of[6], 71), 0)
    win_tile = draw_win_tile(jax.random.fold_in(streams_of[6], 71), 0)
    win_count = draw_win_count(jax.random.fold_in(streams_of[6], 71), 0)
    return {"t2": t2, "v_plus": v_plus, "v_minus": v_minus, "partner": partner, "win_tile": win_tile, "win_count": win_count}


def reference(t2, v_plus, v_minus, partner, win_tile, win_count):
    pair_rows = t2.shape[2]
    block_rows = pair_rows // N_PAIR
    block_id = (jnp.arange(pair_rows) // block_rows).astype(jnp.int32)
    mirror = (jnp.bitwise_xor(block_id, 1) * block_rows + partner).astype(jnp.int32)
    own_values = t2.astype(jnp.float32)
    mirror_values = jnp.take(t2, mirror, axis=2).astype(jnp.float32)
    plus = (own_values + mirror_values).astype(jnp.bfloat16)
    minus = (own_values - mirror_values).astype(jnp.bfloat16)
    contract = (((0, 1), (0, 1)), ((), ()))

    def owner_block(inputs):
        tiles_here, count_here, plus_slab, minus_slab = inputs
        living = (jnp.arange(WIN) < count_here)[:, None, None]
        wplus = jnp.where(living, jnp.take(plus, tiles_here, axis=0), jnp.zeros((), jnp.bfloat16))
        wminus = jnp.where(living, jnp.take(minus, tiles_here, axis=0), jnp.zeros((), jnp.bfloat16))
        first = lax.dot_general(wplus.astype(jnp.float32), plus_slab.astype(jnp.float32), contract)
        second = lax.dot_general(wminus.astype(jnp.float32), minus_slab.astype(jnp.float32), contract)
        return (0.5 * (first + second)).astype(jnp.bfloat16)

    blocks = lax.map(owner_block, (win_tile, win_count, v_plus, v_minus))
    return jnp.transpose(blocks, (1, 0, 2)).reshape(pair_rows, N_TILES * SAB)
```

```python
import functools

import jax
import jax.numpy as jnp
from jax import lax
from jax.experimental import pallas as pl
from jax.experimental.pallas import tpu as pltpu
from jax.sharding import PartitionSpec as P

MESH = pl.DeviceIdType.MESH


def route_plan(win_tile, win_count, per_source, capacity):
    owners, slots = win_tile.shape
    me = lax.axis_index("tiles")
    sources = win_tile // per_source
    offsets = win_tile % per_source
    positions = jnp.arange(slots)
    living = positions[None, :] < win_count[:, None]
    earlier = positions[None, None, :] < positions[None, :, None]
    same = (sources[:, :, None] == sources[:, None, :]) & living[:, None, :] & earlier
    ranked = jnp.sum(same, axis=2, dtype=jnp.int32)
    ranks = jnp.arange(capacity)
    taken = (living & (sources == me))[:, :, None] & (ranked[:, :, None] == ranks)
    send = jnp.sum(jnp.where(taken, offsets[:, :, None], 0), axis=1, dtype=jnp.int32)
    mine = [lax.dynamic_index_in_dim(x, me, 0, keepdims=False) for x in (sources, ranked, living)]
    filled = (
        mine[2][None, None, :]
        & (mine[0][None, None, :] == jnp.arange(owners)[:, None, None])
        & (mine[1][None, None, :] == ranks[None, :, None])
    )
    slot = jnp.sum(jnp.where(filled, positions + 1, 0), axis=2, dtype=jnp.int32) - 1
    return send.reshape(-1), slot.reshape(-1)


def across(me, n, d):
    other, place = 0, 1
    while place < n:
        other = other + ((me // place) % 2 + (d // place) % 2) % 2 * place
        place *= 2
    return other


def kernel(
    n, cap, order,
    send_idx, slot_idx, partner, t2_hbm, vp_hbm, vm_hbm, out_hbm,
    t2, vp, vm, pack, recv, mirror, onehot, vst, wt, acc, staged,
    in_sem, send_sem, recv_sem, fwd_sem, mir_sem, out_sem,
):
    me = lax.axis_index("tiles")
    pair = lax.axis_index("pair")
    sibling = pair + 1 - 2 * (pair % 2)
    tw, rows = t2.shape[1:]
    cols = vp.shape[2]
    depth = cap * tw
    block = 512

    t2_in = pltpu.make_async_copy(t2_hbm, t2, in_sem.at[0])
    t2_in.start()
    vp_in = pltpu.make_async_copy(vp_hbm.at[0], vp, in_sem.at[1])
    vm_in = pltpu.make_async_copy(vm_hbm.at[0], vm, in_sem.at[2])
    vp_in.start()
    vm_in.start()

    barrier = pltpu.get_barrier_semaphore()

    def greet(d, carry):
        pl.semaphore_signal(barrier, inc=1, device_id={"tiles": across(me, n, d)}, device_id_type=MESH)
        return carry

    lax.fori_loop(1, n, greet, 0)
    pl.semaphore_signal(barrier, inc=1, device_id={"pair": sibling}, device_id_type=MESH)
    pl.semaphore_wait(barrier, n)
    t2_in.wait()

    def route(d):
        return pltpu.make_async_remote_copy(
            src_ref=pack.at[d], dst_ref=recv.at[d], send_sem=send_sem.at[d], recv_sem=recv_sem.at[d],
            device_id={"tiles": across(me, n, d)}, device_id_type=MESH,
        )

    def forward(d, src):
        return pltpu.make_async_remote_copy(
            src_ref=src.at[d], dst_ref=mirror.at[d], send_sem=fwd_sem.at[d], recv_sem=mir_sem.at[d],
            device_id={"pair": sibling}, device_id_type=MESH,
        )

    def fill(d):
        owner = across(me, n, d)
        for r in range(cap):
            pack[d, r * tw : (r + 1) * tw] = t2[send_idx[owner * cap + r]]

    def dispatch(d):
        fill(d)
        route(d).start()

    if n <= 8:
        for d in order:
            dispatch(d)
    else:
        lax.fori_loop(1, n, lambda j, c: (dispatch(n - j), c)[1], 0)
    fill(0)
    forward(0, pack).start()

    @pl.loop(0, rows // 128)
    def _(i):
        at = pl.multiple_of(i * 128, 128)
        row = lax.broadcasted_iota(jnp.int32, (128, rows), 0) + at
        onehot[pl.ds(at, 128), :] = (row == partner[...]).astype(jnp.float32).astype(jnp.bfloat16)

    vp_in.wait()
    vm_in.wait()

    def slabs(d):
        source = across(me, n, d)
        for r in range(cap):
            slot = slot_idx[source * cap + r]
            at = jnp.maximum(slot, 0)
            keep = (slot >= 0).astype(jnp.float32).astype(jnp.bfloat16)
            vst[r * tw : (r + 1) * tw, :] = vp[at] * keep
            vst[depth + r * tw : depth + (r + 1) * tw, :] = vm[at] * keep

    def combine(d, src):
        mir = jnp.dot(mirror[d], onehot[...], preferred_element_type=jnp.float32)
        own = src[d].astype(jnp.float32)
        wt[:, :depth] = jnp.transpose(own + mir).astype(jnp.bfloat16)
        wt[:, depth:] = jnp.transpose(own - mir).astype(jnp.bfloat16)

    def product(at):
        return jnp.dot(wt[...], vst[:, pl.ds(at, block)], preferred_element_type=jnp.float32)

    slabs(0)
    forward(0, pack).wait_recv()
    combine(0, pack)

    @pl.loop(0, cols // block)
    def _(i):
        at = pl.multiple_of(i * block, block)
        acc[:, pl.ds(at, block)] = product(at)

    def arrive(d):
        slabs(d)
        route(d).wait_recv()
        forward(d, recv).start()
        forward(d, recv).wait_recv()
        combine(d, recv)

    def add(d):
        arrive(d)

        @pl.loop(0, cols // block)
        def _(i):
            at = pl.multiple_of(i * block, block)
            acc[:, pl.ds(at, block)] += product(at)

    if n <= 8:
        for d in order[:-1]:
            add(d)
        last = order[-1]
    else:
        lax.fori_loop(1, n - 1, lambda j, c: (add(n - j), c)[1], 0)
        last = 1
    arrive(last)
    writes = []
    for i in range(cols // block):
        at = i * block
        staged[:, at : at + block] = (0.5 * (acc[:, at : at + block] + product(at))).astype(jnp.bfloat16)
        write = pltpu.make_async_copy(
            staged.at[:, at : at + block], out_hbm.at[:, at : at + block], out_sem.at[i]
        )
        write.start()
        writes.append(write)

    def settle(d, carry):
        route(d).wait_send()
        forward(d, recv).wait_send()
        return carry

    lax.fori_loop(1, n, settle, 0)
    forward(0, pack).wait_send()
    for write in writes:
        write.wait()


def body(t2, v_plus, v_minus, partner, win_tile, win_count):
    per_source, tw, rows = t2.shape
    n = lax.axis_size("tiles")
    slots, cols = v_plus.shape[1], v_plus.shape[3]
    cap = max(2, (slots + n - 1) // n)
    send, slot = route_plan(win_tile, win_count, per_source, cap)
    order = (7, 1, 6, 2, 5, 3, 4) if n == 8 else tuple(range(n - 1, 0, -1))
    depth = cap * tw
    vmem, smem, hbm = pltpu.VMEM, pltpu.SMEM, pl.ANY
    return pl.pallas_call(
        functools.partial(kernel, n, cap, order),
        out_shape=jax.ShapeDtypeStruct((rows, cols), jnp.bfloat16),
        in_specs=[pl.BlockSpec(memory_space=m) for m in (smem, smem, vmem, hbm, hbm, hbm)],
        out_specs=pl.BlockSpec(memory_space=hbm),
        scratch_shapes=[
            pltpu.VMEM(t2.shape, jnp.bfloat16),
            pltpu.VMEM(v_plus.shape[1:], jnp.bfloat16),
            pltpu.VMEM(v_minus.shape[1:], jnp.bfloat16),
            pltpu.VMEM((n, depth, rows), jnp.bfloat16),
            pltpu.VMEM((n, depth, rows), jnp.bfloat16),
            pltpu.VMEM((n, depth, rows), jnp.bfloat16),
            pltpu.VMEM((rows, rows), jnp.bfloat16),
            pltpu.VMEM((2 * depth, cols), jnp.bfloat16),
            pltpu.VMEM((rows, 2 * depth), jnp.bfloat16),
            pltpu.VMEM((rows, cols), jnp.float32),
            pltpu.VMEM((rows, cols), jnp.bfloat16),
            pltpu.SemaphoreType.DMA((3,)),
            pltpu.SemaphoreType.DMA((n,)),
            pltpu.SemaphoreType.DMA((n,)),
            pltpu.SemaphoreType.DMA((n,)),
            pltpu.SemaphoreType.DMA((n,)),
            pltpu.SemaphoreType.DMA((cols // 512,)),
        ],
        compiler_params=pltpu.CompilerParams(
            collective_id=0, has_side_effects=True, vmem_limit_bytes=56 * 2**20
        ),
        cost_estimate=pl.CostEstimate(
            flops=4 * rows * cols * n * depth, bytes_accessed=16 * 2**20, transcendentals=0
        ),
    )(send, slot, partner.reshape(1, rows), t2, v_plus, v_minus)


def solution(mesh):
    placed = (
        P("tiles", None, "pair"),
        P("tiles", None, None, None),
        P("tiles", None, None, None),
        P("pair"),
        P(),
        P(),
    )
    return jax.shard_map(
        body, mesh=mesh, in_specs=placed, out_specs=P("pair", "tiles"), check_vma=False
    )
```

```python
import functools

import jax
import jax.numpy as jnp
from jax import lax
from jax.experimental import pallas as pl
from jax.experimental.pallas import tpu as pltpu
from jax.sharding import PartitionSpec as P

MESH = pl.DeviceIdType.MESH


def split_tile(tile, per_source):
    if per_source & (per_source - 1) == 0:
        return tile >> (per_source.bit_length() - 1), tile & (per_source - 1)
    return tile // per_source, tile % per_source


def route_plan(win_tile, win_count, per_source, capacity):
    owners, slots = win_tile.shape
    me = lax.axis_index("tiles")
    sources, offsets = split_tile(win_tile, per_source)
    positions = jnp.arange(slots)
    living = positions[None, :] < win_count[:, None]
    earlier = positions[None, None, :] < positions[None, :, None]
    same = (sources[:, :, None] == sources[:, None, :]) & living[:, None, :] & earlier
    ranked = jnp.sum(same, axis=2, dtype=jnp.int32)
    ranks = jnp.arange(capacity)
    taken = (living & (sources == me))[:, :, None] & (ranked[:, :, None] == ranks)
    send = jnp.sum(jnp.where(taken, offsets[:, :, None], 0), axis=1, dtype=jnp.int32)
    mine = [lax.dynamic_index_in_dim(x, me, 0, keepdims=False) for x in (sources, ranked, living)]
    filled = (
        mine[2][None, None, :]
        & (mine[0][None, None, :] == jnp.arange(owners)[:, None, None])
        & (mine[1][None, None, :] == ranks[None, :, None])
    )
    slot = jnp.sum(jnp.where(filled, positions + 1, 0), axis=2, dtype=jnp.int32) - 1
    return send, slot


def across(me, n, d):
    other, place = 0, 1
    while place < n:
        other = other + ((me // place) % 2 + (d // place) % 2) % 2 * place
        place *= 2
    return other


def kernel(
    n, cap, order,
    send_idx, slot_idx, partner, t2, vp_hbm, vm_hbm, acc, wt, vst,
    vp, vm, pack, recv, mirror, onehot,
    in_sem, send_sem, recv_sem, fwd_sem, mir_sem,
):
    me = lax.axis_index("tiles")
    pair = lax.axis_index("pair")
    sibling = pair + 1 - 2 * (pair % 2)
    tw, rows = t2.shape[1:]
    cols = vp.shape[2]
    depth = cap * tw
    block = 512

    vp_in = pltpu.make_async_copy(vp_hbm.at[0], vp, in_sem.at[0])
    vm_in = pltpu.make_async_copy(vm_hbm.at[0], vm, in_sem.at[1])
    vp_in.start()
    vm_in.start()

    barrier = pltpu.get_barrier_semaphore()

    def greet(d, carry):
        pl.semaphore_signal(barrier, inc=1, device_id={"tiles": across(me, n, d)}, device_id_type=MESH)
        return carry

    lax.fori_loop(1, n, greet, 0)
    pl.semaphore_signal(barrier, inc=1, device_id={"pair": sibling}, device_id_type=MESH)
    pl.semaphore_wait(barrier, n)

    def route(d):
        return pltpu.make_async_remote_copy(
            src_ref=pack.at[d], dst_ref=recv.at[d], send_sem=send_sem.at[d], recv_sem=recv_sem.at[d],
            device_id={"tiles": across(me, n, d)}, device_id_type=MESH,
        )

    def forward(d, src):
        return pltpu.make_async_remote_copy(
            src_ref=src.at[d], dst_ref=mirror.at[d], send_sem=fwd_sem.at[d], recv_sem=mir_sem.at[d],
            device_id={"pair": sibling}, device_id_type=MESH,
        )

    def fill(d):
        owner = across(me, n, d)
        for r in range(cap):
            pack[d, r * tw : (r + 1) * tw] = t2[send_idx[owner, r]]

    def dispatch(d):
        fill(d)
        route(d).start()

    if n <= 8:
        for d in order:
            dispatch(d)
    else:
        lax.fori_loop(1, n, lambda j, c: (dispatch(n - j), c)[1], 0)
    fill(0)
    forward(0, pack).start()

    @pl.loop(0, rows // 128)
    def _(i):
        at = pl.multiple_of(i * 128, 128)
        row = lax.broadcasted_iota(jnp.int32, (128, rows), 0) + at
        onehot[pl.ds(at, 128), :] = (row == partner[...]).astype(jnp.float32).astype(jnp.bfloat16)

    vp_in.wait()
    vm_in.wait()

    def slabs(d):
        source = across(me, n, d)
        for r in range(cap):
            slot = slot_idx[source, r]
            at = jnp.maximum(slot, 0)
            keep = (slot >= 0).astype(jnp.float32).astype(jnp.bfloat16)
            vst[r * tw : (r + 1) * tw, :] = vp[at] * keep
            vst[depth + r * tw : depth + (r + 1) * tw, :] = vm[at] * keep

    def combine(d, src):
        mir = jnp.dot(mirror[d], onehot[...], preferred_element_type=jnp.float32)
        own = src[d].astype(jnp.float32)
        wt[:, :depth] = jnp.transpose(own + mir).astype(jnp.bfloat16)
        wt[:, depth:] = jnp.transpose(own - mir).astype(jnp.bfloat16)

    def product(at):
        return jnp.dot(wt[...], vst[:, pl.ds(at, block)], preferred_element_type=jnp.float32)

    slabs(0)
    forward(0, pack).wait_recv()
    combine(0, pack)

    @pl.loop(0, cols // block)
    def _(i):
        at = pl.multiple_of(i * block, block)
        acc[:, pl.ds(at, block)] = product(at)

    def arrive(d):
        slabs(d)
        route(d).wait_recv()
        forward(d, recv).start()
        forward(d, recv).wait_recv()
        combine(d, recv)

    def add(d):
        arrive(d)

        @pl.loop(0, cols // block)
        def _(i):
            at = pl.multiple_of(i * block, block)
            acc[:, pl.ds(at, block)] += product(at)

    if n <= 8:
        for d in order[:-1]:
            add(d)
        last = order[-1]
    else:
        lax.fori_loop(1, n - 1, lambda j, c: (add(n - j), c)[1], 0)
        last = 1
    arrive(last)

    def settle(d, carry):
        route(d).wait_send()
        forward(d, recv).wait_send()
        return carry

    lax.fori_loop(1, n, settle, 0)
    forward(0, pack).wait_send()


def finish(acc, wt, vst, out_hbm, staged, out_sem):
    cols = acc.shape[1]
    block = 256
    writes = []
    for i in range(cols // block):
        at = slice(i * block, (i + 1) * block)
        total = acc[:, at] + jnp.dot(wt[...], vst[:, at], preferred_element_type=jnp.float32)
        staged[:, at] = (0.5 * total).astype(jnp.bfloat16)
        write = pltpu.make_async_copy(staged.at[:, at], out_hbm.at[:, at], out_sem.at[i])
        write.start()
        writes.append(write)
    for write in writes:
        write.wait()


def body(t2, v_plus, v_minus, partner, win_tile, win_count):
    per_source, tw, rows = t2.shape
    n = lax.axis_size("tiles")
    slots, cols = v_plus.shape[1], v_plus.shape[3]
    cap = max(2, (slots + n - 1) // n)
    send, slot = route_plan(win_tile, win_count, per_source, cap)
    order = (7, 1, 6, 2, 5, 3, 4) if n == 8 else tuple(range(n - 1, 0, -1))
    depth = cap * tw
    vmem, smem, hbm = pltpu.VMEM, pltpu.SMEM, pltpu.HBM
    partial, last_t, last_v = pl.pallas_call(
        functools.partial(kernel, n, cap, order),
        out_shape=(
            jax.ShapeDtypeStruct((rows, cols), jnp.float32),
            jax.ShapeDtypeStruct((rows, 2 * depth), jnp.bfloat16),
            jax.ShapeDtypeStruct((2 * depth, cols), jnp.bfloat16),
        ),
        in_specs=[pl.BlockSpec(memory_space=m) for m in (smem, smem, vmem, vmem, hbm, hbm)],
        out_specs=(pl.BlockSpec(memory_space=vmem),) * 3,
        scratch_shapes=[
            pltpu.VMEM(v_plus.shape[1:], jnp.bfloat16),
            pltpu.VMEM(v_minus.shape[1:], jnp.bfloat16),
            pltpu.VMEM((n, depth, rows), jnp.bfloat16),
            pltpu.VMEM((n, depth, rows), jnp.bfloat16),
            pltpu.VMEM((n, depth, rows), jnp.bfloat16),
            pltpu.VMEM((rows, rows), jnp.bfloat16),
            pltpu.SemaphoreType.DMA((2,)),
            pltpu.SemaphoreType.DMA((n,)),
            pltpu.SemaphoreType.DMA((n,)),
            pltpu.SemaphoreType.DMA((n,)),
            pltpu.SemaphoreType.DMA((n,)),
        ],
        compiler_params=pltpu.CompilerParams(
            collective_id=0, has_side_effects=True, vmem_limit_bytes=28 * 2**20
        ),
        cost_estimate=pl.CostEstimate(
            flops=4 * rows * cols * n * depth, bytes_accessed=16 * 2**20, transcendentals=0
        ),
    )(
        send,
        slot,
        partner.reshape(1, rows),
        t2,
        pltpu.with_memory_space_constraint(v_plus, hbm),
        pltpu.with_memory_space_constraint(v_minus, hbm),
    )
    return pl.pallas_call(
        finish,
        out_shape=jax.ShapeDtypeStruct((rows, cols), jnp.bfloat16),
        in_specs=[pl.BlockSpec(memory_space=vmem)] * 3,
        out_specs=pl.BlockSpec(memory_space=hbm),
        scratch_shapes=[
            pltpu.VMEM((rows, cols), jnp.bfloat16),
            pltpu.SemaphoreType.DMA((cols // 256,)),
        ],
        compiler_params=pltpu.CompilerParams(vmem_limit_bytes=16 * 2**20),
        cost_estimate=pl.CostEstimate(
            flops=4 * rows * cols * depth, bytes_accessed=16 * 2**20, transcendentals=0
        ),
    )(partial, last_t, last_v)


def solution(mesh):
    placed = (
        P("tiles", None, "pair"),
        P("tiles", None, None, None),
        P("tiles", None, None, None),
        P("pair"),
        P(),
        P(),
    )
    return jax.shard_map(
        body, mesh=mesh, in_specs=placed, out_specs=P("pair", "tiles"), check_vma=False
    )
```

```python
import functools

import jax
import jax.numpy as jnp
from jax import lax
from jax.experimental import pallas as pl
from jax.experimental.pallas import tpu as pltpu
from jax.sharding import PartitionSpec as P

MESH = pl.DeviceIdType.MESH


def split_tile(tile, per_source):
    if per_source & (per_source - 1) == 0:
        return tile >> (per_source.bit_length() - 1), tile & (per_source - 1)
    return tile // per_source, tile % per_source


def route_plan(win_tile, win_count, per_source, capacity):
    owners, slots = win_tile.shape
    me = lax.axis_index("tiles")
    sources, offsets = split_tile(win_tile, per_source)
    positions = jnp.arange(slots)
    living = positions[None, :] < win_count[:, None]
    earlier = positions[None, None, :] < positions[None, :, None]
    same = (sources[:, :, None] == sources[:, None, :]) & living[:, None, :] & earlier
    ranked = jnp.sum(same, axis=2, dtype=jnp.int32)
    ranks = jnp.arange(capacity)
    taken = (living & (sources == me))[:, :, None] & (ranked[:, :, None] == ranks)
    send = jnp.sum(jnp.where(taken, offsets[:, :, None], 0), axis=1, dtype=jnp.int32)
    mine = [lax.dynamic_index_in_dim(x, me, 0, keepdims=False) for x in (sources, ranked, living)]
    filled = (
        mine[2][None, None, :]
        & (mine[0][None, None, :] == jnp.arange(owners)[:, None, None])
        & (mine[1][None, None, :] == ranks[None, :, None])
    )
    slot = jnp.sum(jnp.where(filled, positions + 1, 0), axis=2, dtype=jnp.int32) - 1
    return send, slot


def across(me, n, d):
    other, place = 0, 1
    while place < n:
        other = other + ((me // place) % 2 + (d // place) % 2) % 2 * place
        place *= 2
    return other


def kernel(
    n, cap, far, near,
    send_idx, slot_idx, partner_hbm, t2_hbm, vp_hbm, vm_hbm, acc, far_wt, far_vst,
    t2, partner, vp, vm, pack, recv, mirror, onehot, near_wt, near_vst,
    in_sem, send_sem, recv_sem, fwd_sem, mir_sem,
):
    me = lax.axis_index("tiles")
    pair = lax.axis_index("pair")
    sibling = pair + 1 - 2 * (pair % 2)
    tw, rows = t2.shape[1:]
    cols = vp.shape[2]
    halves, depth = pack.shape[1:3]
    per_half = cap // halves
    block = 512

    reads = [
        pltpu.make_async_copy(src, dst, in_sem.at[i])
        for i, (src, dst) in enumerate(
            [(t2_hbm, t2), (partner_hbm, partner), (vp_hbm.at[0], vp), (vm_hbm.at[0], vm)]
        )
    ]
    for read in reads:
        read.start()

    barrier = pltpu.get_barrier_semaphore()

    def greet(d, carry):
        pl.semaphore_signal(barrier, inc=1, device_id={"tiles": across(me, n, d)}, device_id_type=MESH)
        return carry

    lax.fori_loop(1, n, greet, 0)
    pl.semaphore_signal(barrier, inc=1, device_id={"pair": sibling}, device_id_type=MESH)
    reads[0].wait()

    def fill(d, h):
        owner = across(me, n, d)
        for r in range(per_half):
            pack[d, h, r * tw : (r + 1) * tw] = t2[send_idx[owner, h * per_half + r]]

    def route(d, h):
        return pltpu.make_async_remote_copy(
            src_ref=pack.at[d, h], dst_ref=recv.at[d, h],
            send_sem=send_sem.at[d, h], recv_sem=recv_sem.at[d, h],
            device_id={"tiles": across(me, n, d)}, device_id_type=MESH,
        )

    def forward(d, h, src):
        return pltpu.make_async_remote_copy(
            src_ref=src.at[d, h], dst_ref=mirror.at[d, h],
            send_sem=fwd_sem.at[d, h], recv_sem=mir_sem.at[d, h],
            device_id={"pair": sibling}, device_id_type=MESH,
        )

    far_pieces = [(d, h) for d in far for h in range(halves)]
    near_pieces = [(d, h) for d in near for h in range(halves)]
    ahead = 2
    if far:
        for piece in far_pieces[:ahead]:
            fill(*piece)
    pl.semaphore_wait(barrier, n)
    if far:
        for piece in far_pieces[:ahead]:
            route(*piece).start()
        for piece in near_pieces[:ahead]:
            fill(*piece)
            route(*piece).start()
        for piece in far_pieces[ahead:] + near_pieces[ahead:]:
            fill(*piece)
    else:
        def dispatch(j, carry):
            for h in range(halves):
                fill(n - j, h)
                route(n - j, h).start()
            return carry

        lax.fori_loop(1, n, dispatch, 0)
    for h in range(halves):
        fill(0, h)
        forward(0, h, pack).start()
    reads[1].wait()

    @pl.loop(0, rows // 128)
    def _(i):
        at = pl.multiple_of(i * 128, 128)
        row = lax.broadcasted_iota(jnp.int32, (128, rows), 0) + at
        onehot[pl.ds(at, 128), :] = (row == partner[...]).astype(jnp.float32).astype(jnp.bfloat16)

    reads[2].wait()
    reads[3].wait()

    def slabs(d, vst):
        source = across(me, n, d)
        for r in range(cap):
            slot = slot_idx[source, r]
            at = jnp.maximum(slot, 0)
            keep = (slot >= 0).astype(jnp.float32).astype(jnp.bfloat16)
            to = r // per_half * 2 * depth + r % per_half * tw
            vst[to : to + tw, :] = vp[at] * keep
            vst[to + depth : to + depth + tw, :] = vm[at] * keep

    def combine(d, h, src, wt):
        mir = jnp.dot(mirror[d, h], onehot[...], preferred_element_type=jnp.float32)
        own = src[d, h].astype(jnp.float32)
        both = jnp.concatenate([own + mir, own - mir], axis=0)
        wt[:, h * 2 * depth : (h + 1) * 2 * depth] = jnp.transpose(both).astype(jnp.bfloat16)

    def add(wt, vst, first=False):
        @pl.loop(0, cols // block)
        def _(i):
            at = pl.ds(pl.multiple_of(i * block, block), block)
            part = jnp.dot(wt[...], vst[:, at], preferred_element_type=jnp.float32)
            acc[:, at] = part if first else acc[:, at] + part

    def receive(d, h):
        route(d, h).wait_recv()
        forward(d, h, recv).start()

    def merge(d, h, wt):
        forward(d, h, recv).wait_recv()
        combine(d, h, recv, wt)

    slabs(0, near_vst)
    for h in range(halves):
        forward(0, h, pack).wait_recv()
        combine(0, h, pack, near_wt)
    add(near_wt, near_vst, True)

    if far:
        for k, (d, h) in enumerate(far_pieces):
            beside = near_pieces[k] if k < len(near_pieces) else None
            if h == 0:
                slabs(d, far_vst)
                if beside:
                    slabs(beside[0], near_vst)
            receive(d, h)
            if k + ahead < len(far_pieces):
                route(d, h).wait_send()
                route(*far_pieces[k + ahead]).start()
            if k + ahead < len(near_pieces):
                route(*near_pieces[k + ahead]).start()
            if beside:
                receive(*beside)
            merge(d, h, far_wt)
            if h == halves - 1 and k < len(far_pieces) - 1:
                add(far_wt, far_vst)
            if beside:
                merge(*beside, near_wt)
                if beside[1] == halves - 1:
                    add(near_wt, near_vst)
        for piece in far_pieces[-ahead:] + near_pieces:
            route(*piece).wait_send()
    else:
        def step(d):
            slabs(d, far_vst)
            for h in range(halves):
                receive(d, h)
                merge(d, h, far_wt)

        def whole_step(j, carry):
            step(n - j)
            add(far_wt, far_vst)
            return carry

        lax.fori_loop(1, n - 1, whole_step, 0)
        step(1)

    def settle(d, carry):
        for h in range(halves):
            if not far:
                route(d, h).wait_send()
            forward(d, h, recv).wait_send()
        return carry

    lax.fori_loop(1, n, settle, 0)
    for h in range(halves):
        forward(0, h, pack).wait_send()


def finish(acc, wt, vst, out_hbm, staged, out_sem):
    cols = acc.shape[1]
    block = 256
    writes = []
    for i in range(cols // block):
        at = slice(i * block, (i + 1) * block)
        total = acc[:, at] + jnp.dot(wt[...], vst[:, at], preferred_element_type=jnp.float32)
        staged[:, at] = (0.5 * total).astype(jnp.bfloat16)
        write = pltpu.make_async_copy(staged.at[:, at], out_hbm.at[:, at], out_sem.at[i])
        write.start()
        writes.append(write)
    for write in writes:
        write.wait()


def body(t2, v_plus, v_minus, partner, win_tile, win_count):
    per_source, tw, rows = t2.shape
    n = lax.axis_size("tiles")
    slots, cols = v_plus.shape[1], v_plus.shape[3]
    cap = max(2, (slots + n - 1) // n)
    send, slot = route_plan(win_tile, win_count, per_source, cap)
    halves = 2 if cap % 2 == 0 and cap * tw >= 128 else 1
    far, near = ((7, 6, 5, 4), (1, 2, 3)) if n == 8 else ((), ())
    depth = cap * tw
    pieces = (n, halves, depth // halves, rows)
    vmem, smem, hbm = pltpu.VMEM, pltpu.SMEM, pltpu.HBM
    partial, last_t, last_v = pl.pallas_call(
        functools.partial(kernel, n, cap, far, near),
        out_shape=(
            jax.ShapeDtypeStruct((rows, cols), jnp.float32),
            jax.ShapeDtypeStruct((rows, 2 * depth), jnp.bfloat16),
            jax.ShapeDtypeStruct((2 * depth, cols), jnp.bfloat16),
        ),
        in_specs=[pl.BlockSpec(memory_space=m) for m in (smem, smem, hbm, hbm, hbm, hbm)],
        out_specs=(pl.BlockSpec(memory_space=vmem),) * 3,
        scratch_shapes=[
            pltpu.VMEM(t2.shape, jnp.bfloat16),
            pltpu.VMEM((1, rows), jnp.int32),
            pltpu.VMEM(v_plus.shape[1:], jnp.bfloat16),
            pltpu.VMEM(v_minus.shape[1:], jnp.bfloat16),
            pltpu.VMEM(pieces, jnp.bfloat16),
            pltpu.VMEM(pieces, jnp.bfloat16),
            pltpu.VMEM(pieces, jnp.bfloat16),
            pltpu.VMEM((rows, rows), jnp.bfloat16),
            pltpu.VMEM((rows, 2 * depth), jnp.bfloat16),
            pltpu.VMEM((2 * depth, cols), jnp.bfloat16),
            pltpu.SemaphoreType.DMA((4,)),
            pltpu.SemaphoreType.DMA((n, halves)),
            pltpu.SemaphoreType.DMA((n, halves)),
            pltpu.SemaphoreType.DMA((n, halves)),
            pltpu.SemaphoreType.DMA((n, halves)),
        ],
        compiler_params=pltpu.CompilerParams(
            collective_id=0, has_side_effects=True, vmem_limit_bytes=30 * 2**20
        ),
        cost_estimate=pl.CostEstimate(
            flops=4 * rows * cols * n * depth, bytes_accessed=16 * 2**20, transcendentals=0
        ),
    )(
        send,
        slot,
        pltpu.with_memory_space_constraint(partner.reshape(1, rows), hbm),
        pltpu.with_memory_space_constraint(t2, hbm),
        pltpu.with_memory_space_constraint(v_plus, hbm),
        pltpu.with_memory_space_constraint(v_minus, hbm),
    )
    return pl.pallas_call(
        finish,
        out_shape=jax.ShapeDtypeStruct((rows, cols), jnp.bfloat16),
        in_specs=[pl.BlockSpec(memory_space=vmem)] * 3,
        out_specs=pl.BlockSpec(memory_space=hbm),
        scratch_shapes=[
            pltpu.VMEM((rows, cols), jnp.bfloat16),
            pltpu.SemaphoreType.DMA((cols // 256,)),
        ],
        compiler_params=pltpu.CompilerParams(vmem_limit_bytes=16 * 2**20),
        cost_estimate=pl.CostEstimate(
            flops=4 * rows * cols * depth, bytes_accessed=16 * 2**20, transcendentals=0
        ),
    )(partial, last_t, last_v)


def solution(mesh):
    placed = (
        P("tiles", None, "pair"),
        P("tiles", None, None, None),
        P("tiles", None, None, None),
        P("pair"),
        P(),
        P(),
    )
    return jax.shard_map(
        body, mesh=mesh, in_specs=placed, out_specs=P("pair", "tiles"), check_vma=False
    )
```

```python
import functools

import jax
import jax.numpy as jnp
from jax import lax
from jax.experimental import pallas as pl
from jax.experimental.pallas import tpu as pltpu
from jax.sharding import PartitionSpec as P

MESH = pl.DeviceIdType.MESH


def split_tile(tile, per_source):
    if per_source & (per_source - 1) == 0:
        return tile >> (per_source.bit_length() - 1), tile & (per_source - 1)
    return tile // per_source, tile % per_source


def route_plan(tiles, row, counts, me, per_source, capacity):
    n, slots = tiles.shape
    none, shift = 2**30, 16
    index = lax.broadcasted_iota(jnp.int32, (n, slots), 0)
    slot = lax.broadcasted_iota(jnp.int32, (n, slots), 1)
    count = jnp.zeros((n, slots), jnp.int32)
    for o in range(n):
        count = jnp.where(index == o, counts[o], count)
    source, offset = split_tile(tiles, per_source)
    sends = jnp.where((source == me) & (slot < count), (slot << shift) + offset, none)
    source, _ = split_tile(row, per_source)
    fills = jnp.where((source == index) & (slot < counts[me]), slot << shift, none)
    keys = jnp.concatenate([sends, fills], axis=0)
    lane = lax.broadcasted_iota(jnp.int32, (2 * n, 128), 1)
    plan = jnp.full((2 * n, 128), none, jnp.int32)
    for r in range(capacity):
        first = jnp.min(keys, axis=1, keepdims=True)
        plan = jnp.where(lane == r, first, plan)
        keys = jnp.where(keys == first, none, keys)
    sending = lax.broadcasted_iota(jnp.int32, (2 * n, 128), 0) < n
    found = jnp.where(sending, plan & (2**shift - 1), plan >> shift)
    return jnp.where(plan == none, jnp.where(sending, 0, -1), found)


def across(me, n, d):
    other, place = 0, 1
    while place < n:
        other = other + ((me // place) % 2 + (d // place) % 2) % 2 * place
        place *= 2
    return other


def kernel(
    n, cap, far, near,
    counts_hbm, win_hbm, partner_hbm, t2_hbm, vp_hbm, vm_hbm, acc, far_wt, far_vst,
    counts, win, plan, plan_idx, t2, partner, vp, vm, pack, recv, mirror, onehot, near_wt, near_vst,
    in_sem, send_sem, recv_sem, fwd_sem, mir_sem,
):
    me = lax.axis_index("tiles")
    pair = lax.axis_index("pair")
    sibling = pair + 1 - 2 * (pair % 2)
    tw, rows = t2.shape[1:]
    cols = vp.shape[2]
    halves, depth = pack.shape[1:3]
    per_half = cap // halves
    block = 512

    reads = [
        pltpu.make_async_copy(src, dst, in_sem.at[i])
        for i, (src, dst) in enumerate(
            [
                (win_hbm, win),
                (t2_hbm, t2),
                (partner_hbm, partner),
                (vp_hbm.at[0], vp),
                (vm_hbm.at[0], vm),
                (counts_hbm, counts),
            ]
        )
    ]
    for read in reads:
        read.start()

    barrier = pltpu.get_barrier_semaphore()

    def greet(d, carry):
        pl.semaphore_signal(barrier, inc=1, device_id={"tiles": across(me, n, d)}, device_id_type=MESH)
        return carry

    lax.fori_loop(1, n, greet, 0)
    pl.semaphore_signal(barrier, inc=1, device_id={"pair": sibling}, device_id_type=MESH)
    reads[0].wait()
    reads[5].wait()
    plan[...] = route_plan(win[...], win[pl.ds(me, 1), :], counts, me, t2.shape[0], cap)
    to_smem = pltpu.make_async_copy(plan, plan_idx, in_sem.at[6])
    to_smem.start()
    to_smem.wait()
    reads[1].wait()

    def fill(d, h):
        owner = across(me, n, d)
        for r in range(per_half):
            pack[d, h, r * tw : (r + 1) * tw] = t2[plan_idx[owner, h * per_half + r]]

    def route(d, h):
        return pltpu.make_async_remote_copy(
            src_ref=pack.at[d, h], dst_ref=recv.at[d, h],
            send_sem=send_sem.at[d, h], recv_sem=recv_sem.at[d, h],
            device_id={"tiles": across(me, n, d)}, device_id_type=MESH,
        )

    def forward(d, h, src):
        return pltpu.make_async_remote_copy(
            src_ref=src.at[d, h], dst_ref=mirror.at[d, h],
            send_sem=fwd_sem.at[d, h], recv_sem=mir_sem.at[d, h],
            device_id={"pair": sibling}, device_id_type=MESH,
        )

    far_pieces = [(d, h) for d in far for h in range(halves)]
    near_pieces = [(d, h) for d in near for h in range(halves)]
    ahead = 2
    if far:
        for piece in far_pieces[:ahead]:
            fill(*piece)
    pl.semaphore_wait(barrier, n)
    if far:
        for piece in far_pieces[:ahead]:
            route(*piece).start()
        for piece in near_pieces[:ahead]:
            fill(*piece)
            route(*piece).start()
        for piece in far_pieces[ahead:] + near_pieces[ahead:]:
            fill(*piece)
    else:
        def dispatch(j, carry):
            for h in range(halves):
                fill(n - j, h)
                route(n - j, h).start()
            return carry

        lax.fori_loop(1, n, dispatch, 0)
    for h in range(halves):
        fill(0, h)
        forward(0, h, pack).start()
    reads[2].wait()

    @pl.loop(0, rows // 128)
    def _(i):
        at = pl.multiple_of(i * 128, 128)
        row = lax.broadcasted_iota(jnp.int32, (128, rows), 0) + at
        onehot[pl.ds(at, 128), :] = (row == partner[...]).astype(jnp.float32).astype(jnp.bfloat16)

    reads[3].wait()
    reads[4].wait()

    def slabs(d, vst):
        source = across(me, n, d)
        for r in range(cap):
            slot = plan_idx[n + source, r]
            at = jnp.maximum(slot, 0)
            keep = (slot >= 0).astype(jnp.float32).astype(jnp.bfloat16)
            to = r // per_half * 2 * depth + r % per_half * tw
            vst[to : to + tw, :] = vp[at] * keep
            vst[to + depth : to + depth + tw, :] = vm[at] * keep

    def combine(d, h, src, wt):
        mir = jnp.dot(mirror[d, h], onehot[...], preferred_element_type=jnp.float32)
        own = src[d, h].astype(jnp.float32)
        both = jnp.concatenate([own + mir, own - mir], axis=0)
        wt[:, h * 2 * depth : (h + 1) * 2 * depth] = jnp.transpose(both).astype(jnp.bfloat16)

    def add(wt, vst, first=False):
        @pl.loop(0, cols // block)
        def _(i):
            at = pl.ds(pl.multiple_of(i * block, block), block)
            part = jnp.dot(wt[...], vst[:, at], preferred_element_type=jnp.float32)
            acc[:, at] = part if first else acc[:, at] + part

    def receive(d, h):
        route(d, h).wait_recv()
        forward(d, h, recv).start()

    def merge(d, h, wt):
        forward(d, h, recv).wait_recv()
        combine(d, h, recv, wt)

    slabs(0, near_vst)
    for h in range(halves):
        forward(0, h, pack).wait_recv()
        combine(0, h, pack, near_wt)
    add(near_wt, near_vst, True)

    if far:
        for k, (d, h) in enumerate(far_pieces):
            beside = near_pieces[k] if k < len(near_pieces) else None
            if h == 0:
                slabs(d, far_vst)
                if beside:
                    slabs(beside[0], near_vst)
            receive(d, h)
            if k + ahead < len(far_pieces):
                route(d, h).wait_send()
                route(*far_pieces[k + ahead]).start()
            if k + ahead < len(near_pieces):
                route(*near_pieces[k + ahead]).start()
            if beside:
                receive(*beside)
            merge(d, h, far_wt)
            if h == halves - 1 and k < len(far_pieces) - 1:
                add(far_wt, far_vst)
            if beside:
                merge(*beside, near_wt)
                if beside[1] == halves - 1:
                    add(near_wt, near_vst)
        for piece in far_pieces[-ahead:] + near_pieces:
            route(*piece).wait_send()
    else:
        def step(d):
            slabs(d, far_vst)
            for h in range(halves):
                receive(d, h)
                merge(d, h, far_wt)

        def whole_step(j, carry):
            step(n - j)
            add(far_wt, far_vst)
            return carry

        lax.fori_loop(1, n - 1, whole_step, 0)
        step(1)

    def settle(d, carry):
        for h in range(halves):
            if not far:
                route(d, h).wait_send()
            forward(d, h, recv).wait_send()
        return carry

    lax.fori_loop(1, n, settle, 0)
    for h in range(halves):
        forward(0, h, pack).wait_send()


def finish(acc, wt, vst, out_hbm, staged, out_sem):
    rows = acc.shape[0]
    block = 256
    writes = []
    for i in range(rows // block):
        at = slice(i * block, (i + 1) * block)
        total = acc[at, :] + jnp.dot(wt[at, :], vst[...], preferred_element_type=jnp.float32)
        staged[at, :] = (0.5 * total).astype(jnp.bfloat16)
        write = pltpu.make_async_copy(staged.at[at, :], out_hbm.at[at, :], out_sem.at[i])
        write.start()
        writes.append(write)
    for write in writes:
        write.wait()


def body(t2, v_plus, v_minus, partner, win_tile, win_count):
    tw, rows = t2.shape[1:]
    n = lax.axis_size("tiles")
    slots, cols = v_plus.shape[1], v_plus.shape[3]
    cap = max(2, (slots + n - 1) // n)
    halves = 2 if cap % 2 == 0 and cap * tw >= 128 else 1
    far, near = ((7, 6, 5, 4), (1, 2, 3)) if n == 8 else ((), ())
    depth = cap * tw
    pieces = (n, halves, depth // halves, rows)
    vmem, hbm = pltpu.VMEM, pltpu.HBM
    partial, last_t, last_v = pl.pallas_call(
        functools.partial(kernel, n, cap, far, near),
        out_shape=(
            jax.ShapeDtypeStruct((rows, cols), jnp.float32),
            jax.ShapeDtypeStruct((rows, 2 * depth), jnp.bfloat16),
            jax.ShapeDtypeStruct((2 * depth, cols), jnp.bfloat16),
        ),
        in_specs=[pl.BlockSpec(memory_space=hbm)] * 6,
        out_specs=(pl.BlockSpec(memory_space=vmem),) * 3,
        scratch_shapes=[
            pltpu.SMEM(win_count.shape, jnp.int32),
            pltpu.VMEM(win_tile.shape, jnp.int32),
            pltpu.VMEM((2 * n, 128), jnp.int32),
            pltpu.SMEM((2 * n, 128), jnp.int32),
            pltpu.VMEM(t2.shape, jnp.bfloat16),
            pltpu.VMEM((1, rows), jnp.int32),
            pltpu.VMEM(v_plus.shape[1:], jnp.bfloat16),
            pltpu.VMEM(v_minus.shape[1:], jnp.bfloat16),
            pltpu.VMEM(pieces, jnp.bfloat16),
            pltpu.VMEM(pieces, jnp.bfloat16),
            pltpu.VMEM(pieces, jnp.bfloat16),
            pltpu.VMEM((rows, rows), jnp.bfloat16),
            pltpu.VMEM((rows, 2 * depth), jnp.bfloat16),
            pltpu.VMEM((2 * depth, cols), jnp.bfloat16),
            pltpu.SemaphoreType.DMA((7,)),
            pltpu.SemaphoreType.DMA((n, halves)),
            pltpu.SemaphoreType.DMA((n, halves)),
            pltpu.SemaphoreType.DMA((n, halves)),
            pltpu.SemaphoreType.DMA((n, halves)),
        ],
        compiler_params=pltpu.CompilerParams(
            collective_id=0, has_side_effects=True, vmem_limit_bytes=30 * 2**20
        ),
        cost_estimate=pl.CostEstimate(
            flops=4 * rows * cols * n * depth, bytes_accessed=16 * 2**20, transcendentals=0
        ),
    )(
        pltpu.with_memory_space_constraint(win_count, hbm),
        pltpu.with_memory_space_constraint(win_tile, hbm),
        pltpu.with_memory_space_constraint(partner.reshape(1, rows), hbm),
        pltpu.with_memory_space_constraint(t2, hbm),
        pltpu.with_memory_space_constraint(v_plus, hbm),
        pltpu.with_memory_space_constraint(v_minus, hbm),
    )
    return pl.pallas_call(
        finish,
        out_shape=jax.ShapeDtypeStruct((rows, cols), jnp.bfloat16),
        in_specs=[pl.BlockSpec(memory_space=vmem)] * 3,
        out_specs=pl.BlockSpec(memory_space=hbm),
        scratch_shapes=[
            pltpu.VMEM((rows, cols), jnp.bfloat16),
            pltpu.SemaphoreType.DMA((rows // 256,)),
        ],
        compiler_params=pltpu.CompilerParams(vmem_limit_bytes=16 * 2**20),
        cost_estimate=pl.CostEstimate(
            flops=4 * rows * cols * depth, bytes_accessed=16 * 2**20, transcendentals=0
        ),
    )(partial, last_t, last_v)


def solution(mesh):
    placed = (
        P("tiles", None, "pair"),
        P("tiles", None, None, None),
        P("tiles", None, None, None),
        P("pair"),
        P(),
        P(),
    )
    return jax.shard_map(
        body, mesh=mesh, in_specs=placed, out_specs=P("pair", "tiles"), check_vma=False
    )
```

```python
import functools

import jax
import jax.numpy as jnp
from jax import lax
from jax.experimental import pallas as pl
from jax.experimental.pallas import tpu as pltpu
from jax.sharding import PartitionSpec as P

MESH = pl.DeviceIdType.MESH


def split_tile(tile, per_source):
    if per_source & (per_source - 1) == 0:
        return tile >> (per_source.bit_length() - 1), tile & (per_source - 1)
    return tile // per_source, tile % per_source


def route_plan(tiles, row, counts, me, per_source, capacity):
    n, slots = tiles.shape
    none, shift = 2**30, 16
    index = lax.broadcasted_iota(jnp.int32, (n, slots), 0)
    slot = lax.broadcasted_iota(jnp.int32, (n, slots), 1)
    count = jnp.zeros((n, slots), jnp.int32)
    for o in range(n):
        count = jnp.where(index == o, counts[o], count)
    source, offset = split_tile(tiles, per_source)
    sends = jnp.where((source == me) & (slot < count), (slot << shift) + offset, none)
    source, _ = split_tile(row, per_source)
    fills = jnp.where((source == index) & (slot < counts[me]), slot << shift, none)
    keys = jnp.concatenate([sends, fills], axis=0)
    lane = lax.broadcasted_iota(jnp.int32, (2 * n, 128), 1)
    plan = jnp.full((2 * n, 128), none, jnp.int32)
    for r in range(capacity):
        first = jnp.min(keys, axis=1, keepdims=True)
        plan = jnp.where(lane == r, first, plan)
        keys = jnp.where(keys == first, none, keys)
    sending = lax.broadcasted_iota(jnp.int32, (2 * n, 128), 0) < n
    found = jnp.where(sending, plan & (2**shift - 1), plan >> shift)
    return jnp.where(plan == none, jnp.where(sending, 0, -1), found)


def across(me, n, d):
    other, place = 0, 1
    while place < n:
        other = other + ((me // place) % 2 + (d // place) % 2) % 2 * place
        place *= 2
    return other


def kernel(
    n, cap, far, near,
    counts_hbm, win_hbm, partner_hbm, t2_hbm, vp_hbm, vm_hbm, acc, far_wt, far_vst,
    counts, win, plan, plan_idx, t2, partner, vp, vm, pack, recv, mirror, onehot, near_wt, near_vst,
    in_sem, send_sem, recv_sem, fwd_sem, mir_sem,
):
    me = lax.axis_index("tiles")
    pair = lax.axis_index("pair")
    sibling = pair + 1 - 2 * (pair % 2)
    tw, rows = t2.shape[1:]
    cols = vp.shape[2]
    halves, depth = pack.shape[1:3]
    per_half = cap // halves
    block = 512

    reads = [
        pltpu.make_async_copy(src, dst, in_sem.at[i])
        for i, (src, dst) in enumerate(
            [
                (win_hbm, win),
                (t2_hbm, t2),
                (partner_hbm, partner),
                (vp_hbm.at[0], vp),
                (vm_hbm.at[0], vm),
                (counts_hbm, counts),
            ]
        )
    ]
    for read in reads:
        read.start()

    barrier = pltpu.get_barrier_semaphore()

    def greet(d, carry):
        pl.semaphore_signal(barrier, inc=1, device_id={"tiles": across(me, n, d)}, device_id_type=MESH)
        return carry

    lax.fori_loop(1, n, greet, 0)
    pl.semaphore_signal(barrier, inc=1, device_id={"pair": sibling}, device_id_type=MESH)
    reads[0].wait()
    reads[5].wait()
    plan[...] = route_plan(win[...], win[pl.ds(me, 1), :], counts, me, t2.shape[0], cap)
    to_smem = pltpu.make_async_copy(plan, plan_idx, in_sem.at[6])
    to_smem.start()
    to_smem.wait()
    reads[1].wait()

    def fill(d, h):
        owner = across(me, n, d)
        for r in range(per_half):
            pack[d, h, r * tw : (r + 1) * tw] = t2[plan_idx[owner, h * per_half + r]]

    def route(d, h):
        return pltpu.make_async_remote_copy(
            src_ref=pack.at[d, h], dst_ref=recv.at[d, h],
            send_sem=send_sem.at[d, h], recv_sem=recv_sem.at[d, h],
            device_id={"tiles": across(me, n, d)}, device_id_type=MESH,
        )

    def forward(d, h, src):
        return pltpu.make_async_remote_copy(
            src_ref=src.at[d, h], dst_ref=mirror.at[d, h],
            send_sem=fwd_sem.at[d, h], recv_sem=mir_sem.at[d, h],
            device_id={"pair": sibling}, device_id_type=MESH,
        )

    far_pieces = [(d, h) for d in far for h in range(halves)]
    near_pieces = [(d, h) for d in near for h in range(halves)]
    ahead, beside_ahead = 3, 2
    if far:
        for piece in far_pieces[:ahead]:
            fill(*piece)
    pl.semaphore_wait(barrier, n)
    if far:
        for piece in far_pieces[:ahead]:
            route(*piece).start()
        for piece in near_pieces[:beside_ahead]:
            fill(*piece)
            route(*piece).start()
        for piece in far_pieces[ahead:] + near_pieces[beside_ahead:]:
            fill(*piece)
    else:
        def dispatch(j, carry):
            for h in range(halves):
                fill(n - j, h)
                route(n - j, h).start()
            return carry

        lax.fori_loop(1, n, dispatch, 0)
    for h in range(halves):
        fill(0, h)
        forward(0, h, pack).start()
    reads[2].wait()

    @pl.loop(0, rows // 128)
    def _(i):
        at = pl.multiple_of(i * 128, 128)
        row = lax.broadcasted_iota(jnp.int32, (128, rows), 0) + at
        onehot[pl.ds(at, 128), :] = (row == partner[...]).astype(jnp.float32).astype(jnp.bfloat16)

    reads[3].wait()
    reads[4].wait()

    def slabs(d, vst):
        source = across(me, n, d)
        for r in range(cap):
            slot = plan_idx[n + source, r]
            at = jnp.maximum(slot, 0)
            keep = (slot >= 0).astype(jnp.float32).astype(jnp.bfloat16)
            to = r // per_half * 2 * depth + r % per_half * tw
            vst[to : to + tw, :] = vp[at] * keep
            vst[to + depth : to + depth + tw, :] = vm[at] * keep

    def combine(d, h, src, wt):
        mir = jnp.dot(mirror[d, h], onehot[...], preferred_element_type=jnp.float32)
        own = src[d, h].astype(jnp.float32)
        both = jnp.concatenate([own + mir, own - mir], axis=0)
        wt[:, h * 2 * depth : (h + 1) * 2 * depth] = jnp.transpose(both).astype(jnp.bfloat16)

    def add(wt, vst, first=False):
        @pl.loop(0, cols // block)
        def _(i):
            at = pl.ds(pl.multiple_of(i * block, block), block)
            part = jnp.dot(wt[...], vst[:, at], preferred_element_type=jnp.float32)
            acc[:, at] = part if first else acc[:, at] + part

    def receive(d, h):
        route(d, h).wait_recv()
        forward(d, h, recv).start()

    def merge(d, h, wt):
        forward(d, h, recv).wait_recv()
        combine(d, h, recv, wt)

    slabs(0, near_vst)
    for h in range(halves):
        forward(0, h, pack).wait_recv()
        combine(0, h, pack, near_wt)
    add(near_wt, near_vst, True)

    if far:
        for k, (d, h) in enumerate(far_pieces):
            beside = near_pieces[k] if k < len(near_pieces) else None
            if h == 0:
                slabs(d, far_vst)
                if beside:
                    slabs(beside[0], near_vst)
            if k + ahead < len(far_pieces):
                route(d, h).wait_send()
                route(*far_pieces[k + ahead]).start()
            if k + beside_ahead < len(near_pieces):
                route(*near_pieces[k + beside_ahead]).start()
            receive(d, h)
            if beside:
                receive(*beside)
            merge(d, h, far_wt)
            if h == halves - 1 and k < len(far_pieces) - 1:
                add(far_wt, far_vst)
            if beside:
                merge(*beside, near_wt)
                if beside[1] == halves - 1:
                    add(near_wt, near_vst)
        for piece in far_pieces[-ahead:] + near_pieces:
            route(*piece).wait_send()
    else:
        def step(d):
            slabs(d, far_vst)
            for h in range(halves):
                receive(d, h)
                merge(d, h, far_wt)

        def whole_step(j, carry):
            step(n - j)
            add(far_wt, far_vst)
            return carry

        lax.fori_loop(1, n - 1, whole_step, 0)
        step(1)

    def settle(d, carry):
        for h in range(halves):
            if not far:
                route(d, h).wait_send()
            forward(d, h, recv).wait_send()
        return carry

    lax.fori_loop(1, n, settle, 0)
    for h in range(halves):
        forward(0, h, pack).wait_send()


def finish(acc, wt, vst, out_hbm, staged, out_sem):
    rows = acc.shape[0]
    block = 256
    writes = []
    for i in range(rows // block):
        at = slice(i * block, (i + 1) * block)
        total = acc[at, :] + jnp.dot(wt[at, :], vst[...], preferred_element_type=jnp.float32)
        staged[at, :] = (0.5 * total).astype(jnp.bfloat16)
        write = pltpu.make_async_copy(staged.at[at, :], out_hbm.at[at, :], out_sem.at[i])
        write.start()
        writes.append(write)
    for write in writes:
        write.wait()


def body(t2, v_plus, v_minus, partner, win_tile, win_count):
    tw, rows = t2.shape[1:]
    n = lax.axis_size("tiles")
    slots, cols = v_plus.shape[1], v_plus.shape[3]
    cap = max(2, (slots + n - 1) // n)
    halves = 2 if cap % 2 == 0 and cap * tw >= 128 else 1
    far, near = ((7, 6, 5, 4), (1, 2, 3)) if n == 8 else ((), ())
    depth = cap * tw
    pieces = (n, halves, depth // halves, rows)
    vmem, hbm = pltpu.VMEM, pltpu.HBM
    partial, last_t, last_v = pl.pallas_call(
        functools.partial(kernel, n, cap, far, near),
        out_shape=(
            jax.ShapeDtypeStruct((rows, cols), jnp.float32),
            jax.ShapeDtypeStruct((rows, 2 * depth), jnp.bfloat16),
            jax.ShapeDtypeStruct((2 * depth, cols), jnp.bfloat16),
        ),
        in_specs=[pl.BlockSpec(memory_space=hbm)] * 6,
        out_specs=(pl.BlockSpec(memory_space=vmem),) * 3,
        scratch_shapes=[
            pltpu.SMEM(win_count.shape, jnp.int32),
            pltpu.VMEM(win_tile.shape, jnp.int32),
            pltpu.VMEM((2 * n, 128), jnp.int32),
            pltpu.SMEM((2 * n, 128), jnp.int32),
            pltpu.VMEM(t2.shape, jnp.bfloat16),
            pltpu.VMEM((1, rows), jnp.int32),
            pltpu.VMEM(v_plus.shape[1:], jnp.bfloat16),
            pltpu.VMEM(v_minus.shape[1:], jnp.bfloat16),
            pltpu.VMEM(pieces, jnp.bfloat16),
            pltpu.VMEM(pieces, jnp.bfloat16),
            pltpu.VMEM(pieces, jnp.bfloat16),
            pltpu.VMEM((rows, rows), jnp.bfloat16),
            pltpu.VMEM((rows, 2 * depth), jnp.bfloat16),
            pltpu.VMEM((2 * depth, cols), jnp.bfloat16),
            pltpu.SemaphoreType.DMA((7,)),
            pltpu.SemaphoreType.DMA((n, halves)),
            pltpu.SemaphoreType.DMA((n, halves)),
            pltpu.SemaphoreType.DMA((n, halves)),
            pltpu.SemaphoreType.DMA((n, halves)),
        ],
        compiler_params=pltpu.CompilerParams(
            collective_id=0, has_side_effects=True, vmem_limit_bytes=30 * 2**20
        ),
        cost_estimate=pl.CostEstimate(
            flops=4 * rows * cols * n * depth, bytes_accessed=16 * 2**20, transcendentals=0
        ),
    )(
        pltpu.with_memory_space_constraint(win_count, hbm),
        pltpu.with_memory_space_constraint(win_tile, hbm),
        pltpu.with_memory_space_constraint(partner.reshape(1, rows), hbm),
        pltpu.with_memory_space_constraint(t2, hbm),
        pltpu.with_memory_space_constraint(v_plus, hbm),
        pltpu.with_memory_space_constraint(v_minus, hbm),
    )
    return pl.pallas_call(
        finish,
        out_shape=jax.ShapeDtypeStruct((rows, cols), jnp.bfloat16),
        in_specs=[pl.BlockSpec(memory_space=vmem)] * 3,
        out_specs=pl.BlockSpec(memory_space=hbm),
        scratch_shapes=[
            pltpu.VMEM((rows, cols), jnp.bfloat16),
            pltpu.SemaphoreType.DMA((rows // 256,)),
        ],
        compiler_params=pltpu.CompilerParams(vmem_limit_bytes=16 * 2**20),
        cost_estimate=pl.CostEstimate(
            flops=4 * rows * cols * depth, bytes_accessed=16 * 2**20, transcendentals=0
        ),
    )(partial, last_t, last_v)


def solution(mesh):
    placed = (
        P("tiles", None, "pair"),
        P("tiles", None, None, None),
        P("tiles", None, None, None),
        P("pair"),
        P(),
        P(),
    )
    return jax.shard_map(
        body, mesh=mesh, in_specs=placed, out_specs=P("pair", "tiles"), check_vma=False
    )
```

```python
import functools

import jax
import jax.numpy as jnp
from jax import lax
from jax.experimental import pallas as pl
from jax.experimental.pallas import tpu as pltpu
from jax.sharding import PartitionSpec as P

MESH = pl.DeviceIdType.MESH


def split_tile(tile, per_source):
    if per_source & (per_source - 1) == 0:
        return tile >> (per_source.bit_length() - 1), tile & (per_source - 1)
    return tile // per_source, tile % per_source


def route_plan(tiles, row, counts, me, per_source, capacity):
    n, slots = tiles.shape
    none, shift = 2**30, 16
    index = lax.broadcasted_iota(jnp.int32, (n, slots), 0)
    slot = lax.broadcasted_iota(jnp.int32, (n, slots), 1)
    count = jnp.zeros((n, slots), jnp.int32)
    for o in range(n):
        count = jnp.where(index == o, counts[o], count)
    source, offset = split_tile(tiles, per_source)
    sends = jnp.where((source == me) & (slot < count), (slot << shift) + offset, none)
    source, _ = split_tile(row, per_source)
    fills = jnp.where((source == index) & (slot < counts[me]), slot << shift, none)
    keys = jnp.concatenate([sends, fills], axis=0)
    lane = lax.broadcasted_iota(jnp.int32, (2 * n, 128), 1)
    plan = jnp.full((2 * n, 128), none, jnp.int32)
    for r in range(capacity):
        first = jnp.min(keys, axis=1, keepdims=True)
        plan = jnp.where(lane == r, first, plan)
        keys = jnp.where(keys == first, none, keys)
    sending = lax.broadcasted_iota(jnp.int32, (2 * n, 128), 0) < n
    found = jnp.where(sending, plan & (2**shift - 1), plan >> shift)
    return jnp.where(plan == none, jnp.where(sending, 0, -1), found)


def across(me, n, d):
    other, place = 0, 1
    while place < n:
        other = other + ((me // place) % 2 + (d // place) % 2) % 2 * place
        place *= 2
    return other


def kernel(
    n, cap, far, near,
    counts_hbm, win_hbm, partner_hbm, t2_hbm, vp_hbm, vm_hbm, acc, far_wt, far_vst,
    counts, win, plan, plan_idx, t2, partner, vp, vm, pack, recv, mirror, onehot, near_wt, near_vst,
    in_sem, send_sem, recv_sem, fwd_sem, mir_sem,
):
    me = lax.axis_index("tiles")
    pair = lax.axis_index("pair")
    sibling = pair + 1 - 2 * (pair % 2)
    tw, rows = t2.shape[1:]
    cols = vp.shape[2]
    halves, depth = pack.shape[1:3]
    per_half = cap // halves
    block = 512

    reads = [
        pltpu.make_async_copy(src, dst, in_sem.at[i])
        for i, (src, dst) in enumerate(
            [
                (win_hbm, win),
                (t2_hbm, t2),
                (partner_hbm, partner),
                (vp_hbm.at[0], vp),
                (vm_hbm.at[0], vm),
                (counts_hbm, counts),
            ]
        )
    ]
    for read in reads:
        read.start()

    barrier = pltpu.get_barrier_semaphore()

    def greet(d, carry):
        pl.semaphore_signal(barrier, inc=1, device_id={"tiles": across(me, n, d)}, device_id_type=MESH)
        return carry

    lax.fori_loop(1, n, greet, 0)
    pl.semaphore_signal(barrier, inc=1, device_id={"pair": sibling}, device_id_type=MESH)
    reads[0].wait()
    reads[5].wait()
    plan[...] = route_plan(win[...], win[pl.ds(me, 1), :], counts, me, t2.shape[0], cap)
    to_smem = pltpu.make_async_copy(plan, plan_idx, in_sem.at[6])
    to_smem.start()
    to_smem.wait()
    reads[1].wait()

    def fill(d, h):
        owner = across(me, n, d)
        for r in range(per_half):
            pack[d, h, r * tw : (r + 1) * tw] = t2[plan_idx[owner, h * per_half + r]]

    def route(d, h):
        return pltpu.make_async_remote_copy(
            src_ref=pack.at[d, h], dst_ref=recv.at[d, h],
            send_sem=send_sem.at[d, h], recv_sem=recv_sem.at[d, h],
            device_id={"tiles": across(me, n, d)}, device_id_type=MESH,
        )

    def forward(d, h, src):
        return pltpu.make_async_remote_copy(
            src_ref=src.at[d, h], dst_ref=mirror.at[d, h],
            send_sem=fwd_sem.at[d, h], recv_sem=mir_sem.at[d, h],
            device_id={"pair": sibling}, device_id_type=MESH,
        )

    far_pieces = [(d, h) for d in far for h in range(halves)]
    near_pieces = [(d, h) for d in near for h in range(halves)]
    ahead = 1
    if far:
        for piece in far_pieces[:ahead]:
            fill(*piece)
    pl.semaphore_wait(barrier, n)
    if far:
        for piece in far_pieces[:ahead]:
            route(*piece).start()
        for piece in near_pieces[:ahead]:
            fill(*piece)
            route(*piece).start()
        for piece in far_pieces[ahead:] + near_pieces[ahead:]:
            fill(*piece)
    else:
        def dispatch(j, carry):
            for h in range(halves):
                fill(n - j, h)
                route(n - j, h).start()
            return carry

        lax.fori_loop(1, n, dispatch, 0)
    for h in range(halves):
        fill(0, h)
        forward(0, h, pack).start()
    reads[2].wait()

    @pl.loop(0, rows // 128)
    def _(i):
        at = pl.multiple_of(i * 128, 128)
        row = lax.broadcasted_iota(jnp.int32, (128, rows), 0) + at
        onehot[pl.ds(at, 128), :] = (row == partner[...]).astype(jnp.float32).astype(jnp.bfloat16)

    reads[3].wait()
    reads[4].wait()

    def slabs(d, vst):
        source = across(me, n, d)
        for r in range(cap):
            slot = plan_idx[n + source, r]
            at = jnp.maximum(slot, 0)
            keep = (slot >= 0).astype(jnp.float32).astype(jnp.bfloat16)
            to = r // per_half * 2 * depth + r % per_half * tw
            vst[to : to + tw, :] = vp[at] * keep
            vst[to + depth : to + depth + tw, :] = vm[at] * keep

    def combine(d, h, src, wt):
        mir = jnp.dot(mirror[d, h], onehot[...], preferred_element_type=jnp.float32)
        own = src[d, h].astype(jnp.float32)
        both = jnp.concatenate([own + mir, own - mir], axis=0)
        wt[:, h * 2 * depth : (h + 1) * 2 * depth] = jnp.transpose(both).astype(jnp.bfloat16)

    def add(wt, vst, first=False):
        @pl.loop(0, cols // block)
        def _(i):
            at = pl.ds(pl.multiple_of(i * block, block), block)
            part = jnp.dot(wt[...], vst[:, at], preferred_element_type=jnp.float32)
            acc[:, at] = part if first else acc[:, at] + part

    def receive(d, h):
        route(d, h).wait_recv()
        forward(d, h, recv).start()

    def merge(d, h, wt):
        forward(d, h, recv).wait_recv()
        combine(d, h, recv, wt)

    slabs(0, near_vst)
    for h in range(halves):
        forward(0, h, pack).wait_recv()
        combine(0, h, pack, near_wt)
    add(near_wt, near_vst, True)

    if far:
        for k, (d, h) in enumerate(far_pieces):
            beside = near_pieces[k] if k < len(near_pieces) else None
            if h == 0:
                slabs(d, far_vst)
                if beside:
                    slabs(beside[0], near_vst)
            receive(d, h)
            if k + ahead < len(far_pieces):
                route(d, h).wait_send()
                route(*far_pieces[k + ahead]).start()
            if k + ahead < len(near_pieces):
                route(*near_pieces[k + ahead]).start()
            if beside:
                receive(*beside)
            merge(d, h, far_wt)
            if h == halves - 1 and k < len(far_pieces) - 1:
                add(far_wt, far_vst)
            if beside:
                merge(*beside, near_wt)
                if beside[1] == halves - 1:
                    add(near_wt, near_vst)
        for piece in far_pieces[-ahead:] + near_pieces:
            route(*piece).wait_send()
    else:
        def step(d):
            slabs(d, far_vst)
            for h in range(halves):
                receive(d, h)
                merge(d, h, far_wt)

        def whole_step(j, carry):
            step(n - j)
            add(far_wt, far_vst)
            return carry

        lax.fori_loop(1, n - 1, whole_step, 0)
        step(1)

    def settle(d, carry):
        for h in range(halves):
            if not far:
                route(d, h).wait_send()
            forward(d, h, recv).wait_send()
        return carry

    lax.fori_loop(1, n, settle, 0)
    for h in range(halves):
        forward(0, h, pack).wait_send()


def finish(acc, wt, vst, out_hbm, staged, out_sem):
    rows = acc.shape[0]
    block = 256
    writes = []
    for i in range(rows // block):
        at = slice(i * block, (i + 1) * block)
        total = acc[at, :] + jnp.dot(wt[at, :], vst[...], preferred_element_type=jnp.float32)
        staged[at, :] = (0.5 * total).astype(jnp.bfloat16)
        write = pltpu.make_async_copy(staged.at[at, :], out_hbm.at[at, :], out_sem.at[i])
        write.start()
        writes.append(write)
    for write in writes:
        write.wait()


def body(t2, v_plus, v_minus, partner, win_tile, win_count):
    tw, rows = t2.shape[1:]
    n = lax.axis_size("tiles")
    slots, cols = v_plus.shape[1], v_plus.shape[3]
    cap = max(2, (slots + n - 1) // n)
    halves = 2 if cap % 2 == 0 and cap * tw >= 128 else 1
    far, near = ((7, 6, 5, 4), (1, 2, 3)) if n == 8 else ((), ())
    depth = cap * tw
    pieces = (n, halves, depth // halves, rows)
    vmem, hbm = pltpu.VMEM, pltpu.HBM
    partial, last_t, last_v = pl.pallas_call(
        functools.partial(kernel, n, cap, far, near),
        out_shape=(
            jax.ShapeDtypeStruct((rows, cols), jnp.float32),
            jax.ShapeDtypeStruct((rows, 2 * depth), jnp.bfloat16),
            jax.ShapeDtypeStruct((2 * depth, cols), jnp.bfloat16),
        ),
        in_specs=[pl.BlockSpec(memory_space=hbm)] * 6,
        out_specs=(pl.BlockSpec(memory_space=vmem),) * 3,
        scratch_shapes=[
            pltpu.SMEM(win_count.shape, jnp.int32),
            pltpu.VMEM(win_tile.shape, jnp.int32),
            pltpu.VMEM((2 * n, 128), jnp.int32),
            pltpu.SMEM((2 * n, 128), jnp.int32),
            pltpu.VMEM(t2.shape, jnp.bfloat16),
            pltpu.VMEM((1, rows), jnp.int32),
            pltpu.VMEM(v_plus.shape[1:], jnp.bfloat16),
            pltpu.VMEM(v_minus.shape[1:], jnp.bfloat16),
            pltpu.VMEM(pieces, jnp.bfloat16),
            pltpu.VMEM(pieces, jnp.bfloat16),
            pltpu.VMEM(pieces, jnp.bfloat16),
            pltpu.VMEM((rows, rows), jnp.bfloat16),
            pltpu.VMEM((rows, 2 * depth), jnp.bfloat16),
            pltpu.VMEM((2 * depth, cols), jnp.bfloat16),
            pltpu.SemaphoreType.DMA((7,)),
            pltpu.SemaphoreType.DMA((n, halves)),
            pltpu.SemaphoreType.DMA((n, halves)),
            pltpu.SemaphoreType.DMA((n, halves)),
            pltpu.SemaphoreType.DMA((n, halves)),
        ],
        compiler_params=pltpu.CompilerParams(
            collective_id=0, has_side_effects=True, vmem_limit_bytes=30 * 2**20
        ),
        cost_estimate=pl.CostEstimate(
            flops=4 * rows * cols * n * depth, bytes_accessed=16 * 2**20, transcendentals=0
        ),
    )(
        pltpu.with_memory_space_constraint(win_count, hbm),
        pltpu.with_memory_space_constraint(win_tile, hbm),
        pltpu.with_memory_space_constraint(partner.reshape(1, rows), hbm),
        pltpu.with_memory_space_constraint(t2, hbm),
        pltpu.with_memory_space_constraint(v_plus, hbm),
        pltpu.with_memory_space_constraint(v_minus, hbm),
    )
    return pl.pallas_call(
        finish,
        out_shape=jax.ShapeDtypeStruct((rows, cols), jnp.bfloat16),
        in_specs=[pl.BlockSpec(memory_space=vmem)] * 3,
        out_specs=pl.BlockSpec(memory_space=hbm),
        scratch_shapes=[
            pltpu.VMEM((rows, cols), jnp.bfloat16),
            pltpu.SemaphoreType.DMA((rows // 256,)),
        ],
        compiler_params=pltpu.CompilerParams(vmem_limit_bytes=16 * 2**20),
        cost_estimate=pl.CostEstimate(
            flops=4 * rows * cols * depth, bytes_accessed=16 * 2**20, transcendentals=0
        ),
    )(partial, last_t, last_v)


def solution(mesh):
    placed = (
        P("tiles", None, "pair"),
        P("tiles", None, None, None),
        P("tiles", None, None, None),
        P("pair"),
        P(),
        P(),
    )
    return jax.shard_map(
        body, mesh=mesh, in_specs=placed, out_specs=P("pair", "tiles"), check_vma=False
    )
```

```python
import functools

import jax
import jax.numpy as jnp
from jax import lax
from jax.experimental import pallas as pl
from jax.experimental.pallas import tpu as pltpu
from jax.sharding import PartitionSpec as P

MESH = pl.DeviceIdType.MESH


def split_tile(tile, per_source):
    if per_source & (per_source - 1) == 0:
        return tile >> (per_source.bit_length() - 1), tile & (per_source - 1)
    return tile // per_source, tile % per_source


def route_plan(tiles, row, counts, me, per_source, capacity):
    n, slots = tiles.shape
    none, shift = 2**30, 16
    index = lax.broadcasted_iota(jnp.int32, (n, slots), 0)
    slot = lax.broadcasted_iota(jnp.int32, (n, slots), 1)
    count = jnp.zeros((n, slots), jnp.int32)
    for o in range(n):
        count = jnp.where(index == o, counts[o], count)
    source, offset = split_tile(tiles, per_source)
    sends = jnp.where((source == me) & (slot < count), (slot << shift) + offset, none)
    source, _ = split_tile(row, per_source)
    fills = jnp.where((source == index) & (slot < counts[me]), slot << shift, none)
    keys = jnp.concatenate([sends, fills], axis=0)
    lane = lax.broadcasted_iota(jnp.int32, (2 * n, 128), 1)
    plan = jnp.full((2 * n, 128), none, jnp.int32)
    for r in range(capacity):
        first = jnp.min(keys, axis=1, keepdims=True)
        plan = jnp.where(lane == r, first, plan)
        keys = jnp.where(keys == first, none, keys)
    sending = lax.broadcasted_iota(jnp.int32, (2 * n, 128), 0) < n
    found = jnp.where(sending, plan & (2**shift - 1), plan >> shift)
    return jnp.where(plan == none, jnp.where(sending, 0, -1), found)


def across(me, n, d):
    other, place = 0, 1
    while place < n:
        other = other + ((me // place) % 2 + (d // place) % 2) % 2 * place
        place *= 2
    return other


def kernel(
    n, cap, far, near,
    counts_hbm, win_hbm, partner_hbm, t2_hbm, vp_hbm, vm_hbm, acc, far_wt, far_vst,
    counts, win, plan, plan_idx, t2, partner, vp, vm, pack, recv, mirror, onehot, near_wt, near_vst,
    in_sem, send_sem, recv_sem, fwd_sem, mir_sem,
):
    me = lax.axis_index("tiles")
    pair = lax.axis_index("pair")
    sibling = pair + 1 - 2 * (pair % 2)
    tw, rows = t2.shape[1:]
    cols = vp.shape[2]
    halves, depth = pack.shape[1:3]
    per_half = cap // halves
    block = 512

    reads = [
        pltpu.make_async_copy(src, dst, in_sem.at[i])
        for i, (src, dst) in enumerate(
            [
                (win_hbm, win),
                (t2_hbm, t2),
                (partner_hbm, partner),
                (vp_hbm.at[0], vp),
                (vm_hbm.at[0], vm),
                (counts_hbm, counts),
            ]
        )
    ]
    for read in reads:
        read.start()

    barrier = pltpu.get_barrier_semaphore()

    def greet(d, carry):
        pl.semaphore_signal(barrier, inc=1, device_id={"tiles": across(me, n, d)}, device_id_type=MESH)
        return carry

    lax.fori_loop(1, n, greet, 0)
    pl.semaphore_signal(barrier, inc=1, device_id={"pair": sibling}, device_id_type=MESH)
    reads[0].wait()
    reads[5].wait()
    plan[...] = route_plan(win[...], win[pl.ds(me, 1), :], counts, me, t2.shape[0], cap)
    to_smem = pltpu.make_async_copy(plan, plan_idx, in_sem.at[6])
    to_smem.start()
    to_smem.wait()
    reads[1].wait()

    def fill(d, h):
        owner = across(me, n, d)
        for r in range(per_half):
            pack[d, h, r * tw : (r + 1) * tw] = t2[plan_idx[owner, h * per_half + r]]

    def route(d, h):
        return pltpu.make_async_remote_copy(
            src_ref=pack.at[d, h], dst_ref=recv.at[d, h],
            send_sem=send_sem.at[d, h], recv_sem=recv_sem.at[d, h],
            device_id={"tiles": across(me, n, d)}, device_id_type=MESH,
        )

    def forward(d, h, src):
        return pltpu.make_async_remote_copy(
            src_ref=src.at[d, h], dst_ref=mirror.at[d, h],
            send_sem=fwd_sem.at[d, h], recv_sem=mir_sem.at[d, h],
            device_id={"pair": sibling}, device_id_type=MESH,
        )

    far_pieces = [(d, h) for d in far for h in range(halves)]
    near_pieces = [(d, h) for d in near for h in range(halves)]
    ahead, beside_ahead = 3, 2
    if far:
        for piece in far_pieces[:ahead]:
            fill(*piece)
    pl.semaphore_wait(barrier, n)
    if far:
        for piece in far_pieces[:ahead]:
            route(*piece).start()
        for piece in near_pieces[:beside_ahead]:
            fill(*piece)
            route(*piece).start()
        for piece in far_pieces[ahead:] + near_pieces[beside_ahead:]:
            fill(*piece)
    else:
        def dispatch(j, carry):
            for h in range(halves):
                fill(n - j, h)
                route(n - j, h).start()
            return carry

        lax.fori_loop(1, n, dispatch, 0)
    for h in range(halves):
        fill(0, h)
        forward(0, h, pack).start()
    reads[2].wait()

    @pl.loop(0, rows // 128)
    def _(i):
        at = pl.multiple_of(i * 128, 128)
        row = lax.broadcasted_iota(jnp.int32, (128, rows), 0) + at
        onehot[pl.ds(at, 128), :] = (row == partner[...]).astype(jnp.float32).astype(jnp.bfloat16)

    reads[3].wait()
    reads[4].wait()

    def slabs(d, vst):
        source = across(me, n, d)
        for r in range(cap):
            slot = plan_idx[n + source, r]
            at = jnp.maximum(slot, 0)
            keep = (slot >= 0).astype(jnp.float32).astype(jnp.bfloat16)
            to = r // per_half * 2 * depth + r % per_half * tw
            vst[to : to + tw, :] = vp[at] * keep
            vst[to + depth : to + depth + tw, :] = vm[at] * keep

    def combine(d, h, src, wt):
        mir = jnp.dot(mirror[d, h], onehot[...], preferred_element_type=jnp.float32)
        own = src[d, h].astype(jnp.float32)
        both = jnp.concatenate([own + mir, own - mir], axis=0)
        wt[:, h * 2 * depth : (h + 1) * 2 * depth] = jnp.transpose(both).astype(jnp.bfloat16)

    def add(wt, vst, first=False):
        @pl.loop(0, cols // block)
        def _(i):
            at = pl.ds(pl.multiple_of(i * block, block), block)
            part = jnp.dot(wt[...], vst[:, at], preferred_element_type=jnp.float32)
            acc[:, at] = part if first else acc[:, at] + part

    def receive(d, h):
        route(d, h).wait_recv()
        forward(d, h, recv).start()

    def merge(d, h, wt):
        forward(d, h, recv).wait_recv()
        combine(d, h, recv, wt)

    slabs(0, near_vst)
    for h in range(halves):
        forward(0, h, pack).wait_recv()
        combine(0, h, pack, near_wt)
    add(near_wt, near_vst, True)

    if far:
        for k, (d, h) in enumerate(far_pieces):
            beside = near_pieces[k] if k < len(near_pieces) else None
            if h == 0:
                slabs(d, far_vst)
                if beside:
                    slabs(beside[0], near_vst)
            receive(d, h)
            if k + ahead < len(far_pieces):
                route(d, h).wait_send()
                route(*far_pieces[k + ahead]).start()
            if k + beside_ahead < len(near_pieces):
                route(*near_pieces[k + beside_ahead]).start()
            if beside:
                receive(*beside)
            merge(d, h, far_wt)
            if h == halves - 1 and k < len(far_pieces) - 1:
                add(far_wt, far_vst)
            if beside:
                merge(*beside, near_wt)
                if beside[1] == halves - 1:
                    add(near_wt, near_vst)
        for piece in far_pieces[-ahead:] + near_pieces:
            route(*piece).wait_send()
    else:
        def step(d):
            slabs(d, far_vst)
            for h in range(halves):
                receive(d, h)
                merge(d, h, far_wt)

        def whole_step(j, carry):
            step(n - j)
            add(far_wt, far_vst)
            return carry

        lax.fori_loop(1, n - 1, whole_step, 0)
        step(1)

    def settle(d, carry):
        for h in range(halves):
            if not far:
                route(d, h).wait_send()
            forward(d, h, recv).wait_send()
        return carry

    lax.fori_loop(1, n, settle, 0)
    for h in range(halves):
        forward(0, h, pack).wait_send()


def finish(acc, wt, vst, out_hbm, staged, out_sem):
    rows = acc.shape[0]
    block = 256
    writes = []
    for i in range(rows // block):
        at = slice(i * block, (i + 1) * block)
        total = acc[at, :] + jnp.dot(wt[at, :], vst[...], preferred_element_type=jnp.float32)
        staged[at, :] = (0.5 * total).astype(jnp.bfloat16)
        write = pltpu.make_async_copy(staged.at[at, :], out_hbm.at[at, :], out_sem.at[i])
        write.start()
        writes.append(write)
    for write in writes:
        write.wait()


def body(t2, v_plus, v_minus, partner, win_tile, win_count):
    tw, rows = t2.shape[1:]
    n = lax.axis_size("tiles")
    slots, cols = v_plus.shape[1], v_plus.shape[3]
    cap = max(2, (slots + n - 1) // n)
    halves = 2 if cap % 2 == 0 and cap * tw >= 128 else 1
    far, near = ((7, 6, 5, 4), (1, 2, 3)) if n == 8 else ((), ())
    depth = cap * tw
    pieces = (n, halves, depth // halves, rows)
    vmem, hbm = pltpu.VMEM, pltpu.HBM
    partial, last_t, last_v = pl.pallas_call(
        functools.partial(kernel, n, cap, far, near),
        out_shape=(
            jax.ShapeDtypeStruct((rows, cols), jnp.float32),
            jax.ShapeDtypeStruct((rows, 2 * depth), jnp.bfloat16),
            jax.ShapeDtypeStruct((2 * depth, cols), jnp.bfloat16),
        ),
        in_specs=[pl.BlockSpec(memory_space=hbm)] * 6,
        out_specs=(pl.BlockSpec(memory_space=vmem),) * 3,
        scratch_shapes=[
            pltpu.SMEM(win_count.shape, jnp.int32),
            pltpu.VMEM(win_tile.shape, jnp.int32),
            pltpu.VMEM((2 * n, 128), jnp.int32),
            pltpu.SMEM((2 * n, 128), jnp.int32),
            pltpu.VMEM(t2.shape, jnp.bfloat16),
            pltpu.VMEM((1, rows), jnp.int32),
            pltpu.VMEM(v_plus.shape[1:], jnp.bfloat16),
            pltpu.VMEM(v_minus.shape[1:], jnp.bfloat16),
            pltpu.VMEM(pieces, jnp.bfloat16),
            pltpu.VMEM(pieces, jnp.bfloat16),
            pltpu.VMEM(pieces, jnp.bfloat16),
            pltpu.VMEM((rows, rows), jnp.bfloat16),
            pltpu.VMEM((rows, 2 * depth), jnp.bfloat16),
            pltpu.VMEM((2 * depth, cols), jnp.bfloat16),
            pltpu.SemaphoreType.DMA((7,)),
            pltpu.SemaphoreType.DMA((n, halves)),
            pltpu.SemaphoreType.DMA((n, halves)),
            pltpu.SemaphoreType.DMA((n, halves)),
            pltpu.SemaphoreType.DMA((n, halves)),
        ],
        compiler_params=pltpu.CompilerParams(
            collective_id=0, has_side_effects=True, vmem_limit_bytes=30 * 2**20
        ),
        cost_estimate=pl.CostEstimate(
            flops=4 * rows * cols * n * depth, bytes_accessed=16 * 2**20, transcendentals=0
        ),
    )(
        pltpu.with_memory_space_constraint(win_count, hbm),
        pltpu.with_memory_space_constraint(win_tile, hbm),
        pltpu.with_memory_space_constraint(partner.reshape(1, rows), hbm),
        pltpu.with_memory_space_constraint(t2, hbm),
        pltpu.with_memory_space_constraint(v_plus, hbm),
        pltpu.with_memory_space_constraint(v_minus, hbm),
    )
    return pl.pallas_call(
        finish,
        out_shape=jax.ShapeDtypeStruct((rows, cols), jnp.bfloat16),
        in_specs=[pl.BlockSpec(memory_space=vmem)] * 3,
        out_specs=pl.BlockSpec(memory_space=hbm),
        scratch_shapes=[
            pltpu.VMEM((rows, cols), jnp.bfloat16),
            pltpu.SemaphoreType.DMA((rows // 256,)),
        ],
        compiler_params=pltpu.CompilerParams(vmem_limit_bytes=16 * 2**20),
        cost_estimate=pl.CostEstimate(
            flops=4 * rows * cols * depth, bytes_accessed=16 * 2**20, transcendentals=0
        ),
    )(partial, last_t, last_v)


def solution(mesh):
    placed = (
        P("tiles", None, "pair"),
        P("tiles", None, None, None),
        P("tiles", None, None, None),
        P("pair"),
        P(),
        P(),
    )
    return jax.shard_map(
        body, mesh=mesh, in_specs=placed, out_specs=P("pair", "tiles"), check_vma=False
    )
```
